1024 devices in a mesh: seq: 64 (over z, x_hi, core), exp: 16 (over y, x_lo).
Axes of the slice: x: 4 (x_hi: 2, x_lo: 2; x = x_hi * 2 + x_lo), y: 8, z: 16, core: 2. Of those that a mesh axis runs over, the one named last changes fastest.
Arguments:
- tokens: bfloat16 [32768, 2048], P('seq'), as said below
- phi: bfloat16 [2048, 1024], P('seq', 'exp'), as said below
- expert_out: bfloat16 [1024, 2048], P('exp'), may hold values from -6 to 6
- slot_in_grad: bfloat16 [1024, 2048], P('exp'), may hold values from -6 to 6
- out_grad: bfloat16 [32768, 2048], P('seq'), may hold values from -6 to 6
Outputs:
- token_grad: bfloat16 [32768, 2048], P('seq', 'exp')
- phi_grad: float32 [2048, 1024], P('seq', 'exp')
- slot_grad: bfloat16 [1024, 2048], P('exp', 'seq')
The draws below stay inside these ranges and needn't reach their ends.
Inputs may be any that keep to these rules, and one draw needn't show every extreme that they name: `tokens`: finite token features. `phi`: entries of order 2048 ** -0.5.
All inputs are finite; a program needn't handle non-finite values.
Results may differ from the reference program's by a relative error of at most 0.02.
Values may be sent and summed in bfloat16 or wider, within the bound.
No kernel may reach another device: no remote copies, remote signals or barrier semaphores. Data moves between devices by JAX's collectives and lax.ppermute only.
A program may use at most 32 MiB of HBM per device.

```python
import jax
import jax.numpy as jnp

D = 2048
SLOTS = 1024
TOKENS = 32768


def shared_columns(key):
    return jax.random.normal(key, (D, SLOTS), jnp.float32)


def draw_phi(key, part):
    base = shared_columns(key)
    return (base * D ** (-0.5)).astype(jnp.bfloat16)


def drawn_rows(base):
    picked = jnp.arange(0, TOKENS, 61)
    order = picked // 61
    column = (order % SLOTS).astype(jnp.int32)
    following = ((column + 1) % SLOTS).astype(jnp.int32)
    target = 100.0 + 200.0 * (order % 7).astype(jnp.float32) / 6.0
    first = jnp.take(base, column, axis=1).T
    second = jnp.take(base, following, axis=1).T
    first_norm = jnp.sum(first * first, axis=1) * D ** (-0.5)
    second_norm = jnp.sum(second * second, axis=1) * D ** (-0.5)
    weight_first = 0.5 * target / first_norm
    weight_second = 0.5 * (target - 2.0) / second_norm
    return (picked, weight_first[:, None] * first + weight_second[:, None] * second)


def draw_tokens(key, part):
    base = shared_columns(key)
    key = jax.random.fold_in(key, 7)
    values = jax.random.normal(key, (TOKENS, D), jnp.float32)
    picked, aligned = drawn_rows(base)
    values = values.at[picked].set(aligned)
    return values.astype(jnp.bfloat16)


def block_scale(stream_key, dims, cuts, least, top_value):
    level, own = 1.0, jax.random.fold_in(stream_key, 6)
    for position, parts in cuts:
        heights = jnp.exp(jax.random.uniform(jax.random.fold_in(own, position), (parts,), jnp.float32, least / len(cuts), top_value / len(cuts)))
        level = level * jnp.repeat(heights, dims[position] // parts).reshape([-1 if axis == position else 1 for axis in range(len(dims))])
    return level


def normal_values(stream_key, extent, width, reach, shards=(), held_as=jnp.bfloat16):
    drawn = width * jax.random.normal(stream_key, extent, jnp.float32)
    if shards:
        drawn = drawn * block_scale(stream_key, extent, shards, -0.22, 0.18)
    return jnp.clip(drawn, -reach, reach).astype(held_as)


def setup_inputs(seed: int = 0) -> dict:
    seeds = jax.random.split(jax.random.key(seed), 6)
    tokens = draw_tokens(jax.random.fold_in(seeds[5], 71), 0)
    phi = draw_phi(jax.random.fold_in(seeds[5], 71), 0)
    expert_out = normal_values(seeds[2], (SLOTS, D), 1.0, 6.0, ((0, 16),))
    slot_in_grad = normal_values(seeds[3], (SLOTS, D), 1.0, 6.0, ((0, 16),))
    out_grad = normal_values(seeds[4], (TOKENS, D), 1.0, 6.0, ((0, 64),))
    return dict(tokens=tokens, phi=phi, expert_out=expert_out, slot_in_grad=slot_in_grad, out_grad=out_grad)


def reference(tokens, phi, expert_out, slot_in_grad, out_grad):
    logits = jnp.dot(tokens, phi, preferred_element_type=jnp.float32)
    col_peak = jnp.max(logits, axis=0, keepdims=True)
    dexp = jnp.exp(logits - col_peak)
    dispatch = dexp / jnp.sum(dexp, axis=0, keepdims=True)
    row_peak = jnp.max(logits, axis=1, keepdims=True)
    cexp = jnp.exp(logits - row_peak)
    combine = cexp / jnp.sum(cexp, axis=1, keepdims=True)
    dispatch_b = dispatch.astype(jnp.bfloat16)
    combine_b = combine.astype(jnp.bfloat16)
    slot_grad = jnp.dot(combine_b.T, out_grad, preferred_element_type=jnp.float32).astype(jnp.bfloat16)
    comb_grad = jnp.dot(out_grad, expert_out.T, preferred_element_type=jnp.float32)
    disp_grad = jnp.dot(tokens, slot_in_grad.T, preferred_element_type=jnp.float32)
    row_dot = jnp.sum(combine * comb_grad, axis=1, keepdims=True)
    col_dot = jnp.sum(dispatch * disp_grad, axis=0, keepdims=True)
    logit_grad = (combine * (comb_grad - row_dot) + dispatch * (disp_grad - col_dot)).astype(jnp.bfloat16)
    phi_grad = jnp.dot(tokens.T, logit_grad, preferred_element_type=jnp.float32)
    token_grad = (jnp.dot(dispatch_b, slot_in_grad, preferred_element_type=jnp.float32)
                  + jnp.dot(logit_grad, phi.T, preferred_element_type=jnp.float32)).astype(jnp.bfloat16)
    return token_grad, phi_grad, slot_grad
```

```python
import jax
import jax.numpy as jnp
from jax import lax
from jax.sharding import PartitionSpec as P

BF = jnp.bfloat16
F32 = jnp.float32


def gather_blocks(block, axis, n):
    spread = jnp.broadcast_to(block[None], (n,) + block.shape)
    return lax.all_to_all(spread, axis, 0, 0, tiled=True)


def merge_stats(got, axis):
    peak, total, dot = got[:, 0], got[:, 1], got[:, 2]
    top = jnp.max(peak, axis=0)
    scale = jnp.exp(peak - top[None, :])
    total = jnp.sum(total * scale, axis=0)
    dot = jnp.sum(dot * scale, axis=0)
    return top, total, dot / total


def make_per_device(n_seq, n_exp):
    def per_device(tokens, phi, expert_out, slot_in_grad, out_grad):
        rows, width = tokens.shape
        slots = expert_out.shape[0]
        phi_full = gather_blocks(phi, "seq", n_seq).reshape(width, slots)

        logits = jnp.dot(tokens, phi_full, preferred_element_type=F32)
        disp_grad = lax.dot_general(
            tokens, slot_in_grad, (((1,), (1,)), ((), ())), preferred_element_type=F32
        )
        comb_grad = lax.dot_general(
            out_grad, expert_out, (((1,), (1,)), ((), ())), preferred_element_type=F32
        )

        row_top = jnp.max(logits, axis=1)
        row_exp = jnp.exp(logits - row_top[:, None])
        row_stats = jnp.stack(
            [row_top, jnp.sum(row_exp, axis=1), jnp.sum(row_exp * comb_grad, axis=1)]
        )
        col_top = jnp.max(logits, axis=0)
        col_exp = jnp.exp(logits - col_top[None, :])
        col_stats = jnp.stack(
            [col_top, jnp.sum(col_exp, axis=0), jnp.sum(col_exp * disp_grad, axis=0)]
        )

        row_got = gather_blocks(row_stats, "exp", n_exp)
        row_peak, row_total, row_dot = merge_stats(row_got, "exp")
        col_got = gather_blocks(col_stats, "seq", n_seq)
        col_peak, col_total, col_dot = merge_stats(col_got, "seq")

        combine = jnp.exp(logits - row_peak[:, None]) / row_total[:, None]
        dispatch = jnp.exp(logits - col_peak[None, :]) / col_total[None, :]
        dispatch_b = dispatch.astype(BF)
        combine_b = combine.astype(BF)
        logit_grad = (
            combine * (comb_grad - row_dot[:, None]) + dispatch * (disp_grad - col_dot[None, :])
        ).astype(BF)

        partial = jnp.dot(dispatch_b, slot_in_grad, preferred_element_type=F32)
        partial = partial + lax.dot_general(
            logit_grad, phi_full, (((1,), (1,)), ((), ())), preferred_element_type=F32
        )
        token_grad = lax.psum_scatter(
            partial.astype(BF), "exp", scatter_dimension=1, tiled=True
        )

        slot_term = lax.dot_general(
            out_grad, combine_b, (((0,), (0,)), ((), ())), preferred_element_type=F32
        ).astype(BF)
        phi_term = lax.dot_general(
            tokens, logit_grad, (((0,), (0,)), ((), ())), preferred_element_type=F32
        ).astype(BF)
        both = jnp.stack(
            [slot_term.reshape(n_seq, -1, slots), phi_term.reshape(n_seq, -1, slots)], axis=1
        )
        got = lax.all_to_all(both, "seq", 0, 0, tiled=True)
        total = jnp.sum(got.astype(F32), axis=0)
        slot_grad = total[0].T.astype(BF)
        phi_grad = total[1]
        return (token_grad, phi_grad, slot_grad)

    return per_device


def solution(mesh):
    return jax.shard_map(
        make_per_device(mesh.shape["seq"], mesh.shape["exp"]),
        mesh=mesh,
        in_specs=(P("seq", None), P("seq", "exp"), P("exp", None), P("exp", None), P("seq", None)),
        out_specs=(P("seq", "exp"), P("seq", "exp"), P("exp", "seq")),
        check_vma=False,
    )
```

```python
import jax
import jax.numpy as jnp
from jax import lax
from jax.experimental import pallas as pl
from jax.experimental.pallas import tpu as pltpu
from jax.sharding import Mesh
from jax.sharding import PartitionSpec as P

BF = jnp.bfloat16
F32 = jnp.float32
EXP = ("y", "xl")
SWAP = [(0, 1), (1, 0)]


def gather_blocks(block, axis, n):
    spread = jnp.broadcast_to(block[None], (n,) + block.shape)
    return lax.all_to_all(spread, axis, 0, 0, tiled=True)


def merge_stats(got):
    peak, total, dot = got[:, 0], got[:, 1], got[:, 2]
    top = jnp.max(peak, axis=0)
    scale = jnp.exp(peak - top[None, :])
    total = jnp.sum(total * scale, axis=0)
    dot = jnp.sum(dot * scale, axis=0)
    return top, total, dot / total


def weights_kernel(place_ref, sig_ref, phi_ref, own_ref, lent_ref):
    wide = own_ref.shape[1]
    slots = sig_ref.shape[0]
    first = place_ref[0] == 0
    for top, part in ((0, sig_ref[...]), (slots, phi_ref[...].T)):
        even, odd = part[:, :wide], part[:, wide:]
        own_ref[top : top + slots] = jnp.where(first, even, odd)
        lent_ref[top : top + slots] = jnp.where(first, odd, even)


def split_weights(place, sig, phi_full, n, wide):
    slots, width = sig.shape
    out = jax.ShapeDtypeStruct((2 * slots, n * wide), BF)
    spec = pl.BlockSpec((2 * slots, wide), lambda i: (0, i))
    return pl.pallas_call(
        weights_kernel,
        grid=(n,),
        in_specs=[
            pl.BlockSpec(memory_space=pltpu.SMEM),
            pl.BlockSpec((slots, 2 * wide), lambda i: (0, i)),
            pl.BlockSpec((2 * wide, slots), lambda i: (i, 0)),
        ],
        out_specs=[spec, spec],
        out_shape=[out, out],
        cost_estimate=pl.CostEstimate(
            flops=4 * slots * width, bytes_accessed=8 * slots * width, transcendentals=0
        ),
        compiler_params=pltpu.CompilerParams(vmem_limit_bytes=32 * 1024 * 1024),
    )(place[None], sig, phi_full)


def blocks_kernel(own_ref, far_ref, own_w_ref, far_w_ref, out_ref):
    acc = jnp.dot(own_ref[...], own_w_ref[...], preferred_element_type=F32)
    acc = acc + jnp.dot(far_ref[...], far_w_ref[...], preferred_element_type=F32)
    out_ref[0] = acc.astype(BF)


def column_blocks(own, far, own_w, far_w, n, wide):
    rows, depth = own.shape
    whole = pl.BlockSpec((rows, depth), lambda i: (0, 0))
    part = pl.BlockSpec((depth, wide), lambda i: (0, i))
    return pl.pallas_call(
        blocks_kernel,
        grid=(n,),
        in_specs=[whole, whole, part, part],
        out_specs=pl.BlockSpec((1, rows, wide), lambda i: (i, 0, 0)),
        out_shape=jax.ShapeDtypeStruct((n, rows, wide), BF),
        cost_estimate=pl.CostEstimate(
            flops=4 * n * rows * depth * wide,
            bytes_accessed=2 * (2 * rows * depth + 2 * n * depth * wide + n * rows * wide),
            transcendentals=0,
        ),
        compiler_params=pltpu.CompilerParams(vmem_limit_bytes=32 * 1024 * 1024),
    )(own, far, own_w, far_w)


def make_per_device(n_seq, n_y):
    def per_device(tokens, phi, expert_out, slot_in_grad, out_grad):
        rows, width = tokens.shape
        slots = expert_out.shape[0]
        wide = width // (2 * n_y)
        half = phi.shape[0] // 2
        packed = jnp.concatenate([phi[:half], phi[half:]], axis=1)
        got_phi = gather_blocks(packed, "seq", n_seq)
        phi_full = jnp.concatenate([got_phi[:, :, :slots], got_phi[:, :, slots:]], axis=1)
        phi_full = phi_full.reshape(width, slots)

        logits = jnp.dot(tokens, phi_full, preferred_element_type=F32)
        disp_grad = lax.dot_general(
            tokens, slot_in_grad, (((1,), (1,)), ((), ())), preferred_element_type=F32
        )
        comb_grad = lax.dot_general(
            out_grad, expert_out, (((1,), (1,)), ((), ())), preferred_element_type=F32
        )

        place = lax.axis_index("xl").astype(jnp.int32)
        own_w, lent_w = split_weights(place, slot_in_grad, phi_full, n_y, wide)
        far_w = lax.ppermute(lent_w, "xl", SWAP)

        row_top = jnp.max(logits, axis=1)
        row_exp = jnp.exp(logits - row_top[:, None])
        row_stats = jnp.stack(
            [row_top, jnp.sum(row_exp, axis=1), jnp.sum(row_exp * comb_grad, axis=1)]
        )
        col_top = jnp.max(logits, axis=0)
        col_exp = jnp.exp(logits - col_top[None, :])
        col_stats = jnp.stack(
            [col_top, jnp.sum(col_exp, axis=0), jnp.sum(col_exp * disp_grad, axis=0)]
        )

        row_got = gather_blocks(row_stats, EXP, 2 * n_y)
        row_got, far_w = lax.optimization_barrier((row_got, far_w))
        row_peak, row_total, row_dot = merge_stats(row_got)
        col_got = gather_blocks(col_stats, "seq", n_seq)
        col_peak, col_total, col_dot = merge_stats(col_got)

        combine = jnp.exp(logits - row_peak[:, None]) / row_total[:, None]
        dispatch = jnp.exp(logits - col_peak[None, :]) / col_total[None, :]
        combine_b = combine.astype(BF)
        logit_grad = (
            combine * (comb_grad - row_dot[:, None]) + dispatch * (disp_grad - col_dot[None, :])
        ).astype(BF)

        own = jnp.concatenate([dispatch.astype(BF), logit_grad], axis=1)
        own, logit_grad, combine_b = lax.optimization_barrier((own, logit_grad, combine_b))
        far = lax.ppermute(own, "xl", SWAP)
        slot_term = lax.dot_general(
            out_grad, combine_b, (((0,), (0,)), ((), ())), preferred_element_type=F32
        ).astype(BF)

        partial = column_blocks(own, far, own_w, far_w, n_y, wide)
        partial, logit_grad, slot_term = lax.optimization_barrier((partial, logit_grad, slot_term))
        token_grad = lax.psum_scatter(
            partial.reshape(n_y * rows, wide), "y", scatter_dimension=0, tiled=True
        )
        phi_term = lax.dot_general(
            tokens, logit_grad, (((0,), (0,)), ((), ())), preferred_element_type=F32
        ).astype(BF)
        both = jnp.concatenate([phi_term, slot_term], axis=1)
        got = lax.all_to_all(both.reshape(n_seq, -1, 2 * slots), "seq", 0, 0, tiled=True)
        total = jnp.sum(got.astype(F32), axis=0)
        phi_grad = total[:, :slots]
        slot_grad = total[:, slots:].T.astype(BF)
        return (token_grad, phi_grad, slot_grad)

    return per_device


def solution(mesh):
    n_seq, n_exp = mesh.devices.shape
    n_y = n_exp // 2
    fine = Mesh(mesh.devices.reshape(n_seq, n_y, 2), ("seq", "y", "xl"))
    return jax.shard_map(
        make_per_device(n_seq, n_y),
        mesh=fine,
        in_specs=(P("seq", None), P("seq", EXP), P(EXP, None), P(EXP, None), P("seq", None)),
        out_specs=(P("seq", EXP), P("seq", EXP), P(EXP, "seq")),
        check_vma=False,
    )
```

```python
import jax
import jax.numpy as jnp
from jax import lax
from jax.experimental import pallas as pl
from jax.experimental.pallas import tpu as pltpu
from jax.sharding import Mesh
from jax.sharding import PartitionSpec as P

BF = jnp.bfloat16
F32 = jnp.float32
EXP = ("y", "xl")
SWAP = [(0, 1), (1, 0)]


def gather_blocks(block, axis, n):
    spread = jnp.broadcast_to(block[None], (n,) + block.shape)
    return lax.all_to_all(spread, axis, 0, 0, tiled=True)


def merge_stats(got):
    peak, total, dot = got[:, 0], got[:, 1], got[:, 2]
    top = jnp.max(peak, axis=0)
    scale = jnp.exp(peak - top[None, :])
    total = jnp.sum(total * scale, axis=0)
    dot = jnp.sum(dot * scale, axis=0)
    return top, total, dot / total


def weights_kernel(place_ref, sig_ref, phi_ref, own_ref, lent_ref):
    wide = own_ref.shape[1]
    slots = sig_ref.shape[0]
    first = place_ref[0] == 0
    for top, part in ((0, sig_ref[...]), (slots, phi_ref[...].T)):
        even, odd = part[:, :wide], part[:, wide:]
        own_ref[top : top + slots] = jnp.where(first, even, odd)
        lent_ref[top : top + slots] = jnp.where(first, odd, even)


def split_weights(place, sig, phi_full, n, wide):
    slots, width = sig.shape
    out = jax.ShapeDtypeStruct((2 * slots, n * wide), BF)
    spec = pl.BlockSpec((2 * slots, wide), lambda i, at: (0, i))
    return pl.pallas_call(
        weights_kernel,
        grid_spec=pltpu.PrefetchScalarGridSpec(
            num_scalar_prefetch=1,
            grid=(n,),
            in_specs=[
                pl.BlockSpec((slots, 2 * wide), lambda i, at: (0, lax.rem(i + at[1], n))),
                pl.BlockSpec((2 * wide, slots), lambda i, at: (lax.rem(i + at[1], n), 0)),
            ],
            out_specs=[spec, spec],
        ),
        out_shape=[out, out],
        cost_estimate=pl.CostEstimate(
            flops=4 * slots * width, bytes_accessed=8 * slots * width, transcendentals=0
        ),
        compiler_params=pltpu.CompilerParams(vmem_limit_bytes=32 * 1024 * 1024),
    )(place, sig, phi_full)


def blocks_kernel(own_ref, far_ref, own_w_ref, far_w_ref, *out_refs):
    own, far = own_ref[...], far_ref[...]
    for i, out_ref in enumerate(out_refs):
        wide = out_ref.shape[1]
        at = slice(i * wide, (i + 1) * wide)
        acc = jnp.dot(own, own_w_ref[:, at], preferred_element_type=F32)
        acc = acc + jnp.dot(far, far_w_ref[:, at], preferred_element_type=F32)
        out_ref[...] = acc.astype(BF)


def column_blocks(own, far, own_w, far_w, n, wide):
    rows, depth = own.shape
    return pl.pallas_call(
        blocks_kernel,
        out_shape=[jax.ShapeDtypeStruct((rows, wide), BF)] * n,
        cost_estimate=pl.CostEstimate(
            flops=4 * n * rows * depth * wide,
            bytes_accessed=2 * (2 * rows * depth + 2 * n * depth * wide + n * rows * wide),
            transcendentals=0,
        ),
        compiler_params=pltpu.CompilerParams(vmem_limit_bytes=32 * 1024 * 1024),
    )(own, far, own_w, far_w)


def make_per_device(n_seq, n_y):
    def per_device(tokens, phi, expert_out, slot_in_grad, out_grad):
        rows, width = tokens.shape
        slots = expert_out.shape[0]
        wide = width // (2 * n_y)
        half = phi.shape[0] // 2
        packed = jnp.concatenate([phi[:half], phi[half:]], axis=1)
        got_phi = gather_blocks(packed, "seq", n_seq)
        phi_full = jnp.concatenate([got_phi[:, :, :slots], got_phi[:, :, slots:]], axis=1)
        phi_full = phi_full.reshape(width, slots)

        logits = jnp.dot(tokens, phi_full, preferred_element_type=F32)
        disp_grad = lax.dot_general(
            tokens, slot_in_grad, (((1,), (1,)), ((), ())), preferred_element_type=F32
        )
        comb_grad = lax.dot_general(
            out_grad, expert_out, (((1,), (1,)), ((), ())), preferred_element_type=F32
        )

        place = jnp.stack([lax.axis_index("xl"), lax.axis_index("y")]).astype(jnp.int32)
        own_w, lent_w = split_weights(place, slot_in_grad, phi_full, n_y, wide)
        far_w = lax.ppermute(lent_w, "xl", SWAP)

        row_top = jnp.max(logits, axis=1)
        row_exp = jnp.exp(logits - row_top[:, None])
        row_stats = jnp.stack(
            [row_top, jnp.sum(row_exp, axis=1), jnp.sum(row_exp * comb_grad, axis=1)]
        )
        col_top = jnp.max(logits, axis=0)
        col_exp = jnp.exp(logits - col_top[None, :])
        col_stats = jnp.stack(
            [col_top, jnp.sum(col_exp, axis=0), jnp.sum(col_exp * disp_grad, axis=0)]
        )

        row_got = gather_blocks(row_stats, EXP, 2 * n_y)
        row_got, far_w = lax.optimization_barrier((row_got, far_w))
        row_peak, row_total, row_dot = merge_stats(row_got)
        col_got = gather_blocks(col_stats, "seq", n_seq)
        col_peak, col_total, col_dot = merge_stats(col_got)

        combine = jnp.exp(logits - row_peak[:, None]) / row_total[:, None]
        dispatch = jnp.exp(logits - col_peak[None, :]) / col_total[None, :]
        combine_b = combine.astype(BF)
        logit_grad = (
            combine * (comb_grad - row_dot[:, None]) + dispatch * (disp_grad - col_dot[None, :])
        ).astype(BF)

        own = jnp.concatenate([dispatch.astype(BF), logit_grad], axis=1)
        own, logit_grad, combine_b = lax.optimization_barrier((own, logit_grad, combine_b))
        far = lax.ppermute(own, "xl", SWAP)
        slot_term = lax.dot_general(
            out_grad, combine_b, (((0,), (0,)), ((), ())), preferred_element_type=F32
        ).astype(BF)

        phi_term = lax.dot_general(
            tokens, logit_grad, (((0,), (0,)), ((), ())), preferred_element_type=F32
        ).astype(BF)
        both = jnp.concatenate([phi_term, slot_term], axis=1)
        got = lax.all_to_all(both.reshape(n_seq, -1, 2 * slots), "seq", 0, 0, tiled=True)

        blocks = column_blocks(own, far, own_w, far_w, n_y, wide)
        token_sum = blocks[0].astype(F32)
        for i in range(1, n_y):
            turn = [(j, (j + i) % n_y) for j in range(n_y)]
            token_sum = token_sum + lax.ppermute(blocks[i], "y", turn).astype(F32)
        token_grad = token_sum.astype(BF)

        total = jnp.sum(got.astype(F32), axis=0)
        phi_grad = total[:, :slots]
        slot_grad = total[:, slots:].T.astype(BF)
        return (token_grad, phi_grad, slot_grad)

    return per_device


def solution(mesh):
    n_seq, n_exp = mesh.devices.shape
    n_y = n_exp // 2
    fine = Mesh(mesh.devices.reshape(n_seq, n_y, 2), ("seq", "y", "xl"))
    return jax.shard_map(
        make_per_device(n_seq, n_y),
        mesh=fine,
        in_specs=(P("seq", None), P("seq", EXP), P(EXP, None), P(EXP, None), P("seq", None)),
        out_specs=(P("seq", EXP), P("seq", EXP), P(EXP, "seq")),
        check_vma=False,
    )
```

```python
import jax
import jax.numpy as jnp
from jax import lax
from jax.experimental import pallas as pl
from jax.experimental.pallas import tpu as pltpu
from jax.sharding import PartitionSpec as P

BF = jnp.bfloat16
F32 = jnp.float32
GROUP = 4


def gather_blocks(block, axis, n):
    spread = jnp.broadcast_to(block[None], (n,) + block.shape)
    return lax.all_to_all(spread, axis, 0, 0, tiled=True)


def merge_stats(got):
    peak, total, dot = got[:, 0], got[:, 1], got[:, 2]
    top = jnp.max(peak, axis=0)
    scale = jnp.exp(peak - top[None, :])
    total = jnp.sum(total * scale, axis=0)
    dot = jnp.sum(dot * scale, axis=0)
    return top, total, dot / total


def weights_kernel(place_ref, sig_ref, phi_ref, *out_refs):
    slots = sig_ref.shape[0]
    wide = out_refs[0].shape[1]
    for k, out_ref in enumerate(out_refs):
        block = jnp.bitwise_xor(place_ref[0], k)
        at = pl.ds(pl.multiple_of(block * wide, wide), wide)
        out_ref[:slots] = sig_ref[:, at]
        out_ref[slots:] = phi_ref[at, :].T


def split_weights(place, sig, phi_full, n, wide):
    slots, width = sig.shape
    spec = pl.BlockSpec((2 * slots, wide), lambda i, at: (0, i))
    return pl.pallas_call(
        weights_kernel,
        grid_spec=pltpu.PrefetchScalarGridSpec(
            num_scalar_prefetch=1,
            grid=(n,),
            in_specs=[
                pl.BlockSpec((slots, GROUP * wide), lambda i, at: (0, lax.rem(i + at[1], n))),
                pl.BlockSpec((GROUP * wide, slots), lambda i, at: (lax.rem(i + at[1], n), 0)),
            ],
            out_specs=[spec] * GROUP,
        ),
        out_shape=[jax.ShapeDtypeStruct((2 * slots, n * wide), BF)] * GROUP,
        cost_estimate=pl.CostEstimate(
            flops=4 * slots * width, bytes_accessed=8 * slots * width, transcendentals=0
        ),
        compiler_params=pltpu.CompilerParams(vmem_limit_bytes=32 * 1024 * 1024),
    )(place, sig, phi_full)


def blocks_kernel(*refs):
    factors, weights, out_refs = refs[:GROUP], refs[GROUP : 2 * GROUP], refs[2 * GROUP :]
    for i, out_ref in enumerate(out_refs):
        wide = out_ref.shape[1]
        at = slice(i * wide, (i + 1) * wide)
        acc = jnp.dot(factors[0][...], weights[0][:, at], preferred_element_type=F32)
        for f, w in zip(factors[1:], weights[1:]):
            acc = acc + jnp.dot(f[...], w[:, at], preferred_element_type=F32)
        out_ref[...] = acc.astype(BF)


def column_blocks(factors, weights, n, wide):
    rows, depth = factors[0].shape
    return pl.pallas_call(
        blocks_kernel,
        out_shape=[jax.ShapeDtypeStruct((rows, wide), BF)] * n,
        cost_estimate=pl.CostEstimate(
            flops=2 * GROUP * n * rows * depth * wide,
            bytes_accessed=2 * (GROUP * depth * (rows + n * wide) + n * rows * wide),
            transcendentals=0,
        ),
        compiler_params=pltpu.CompilerParams(vmem_limit_bytes=32 * 1024 * 1024),
    )(*factors, *weights)


def make_per_device(n_seq, n_exp):
    groups = n_exp // GROUP

    def swap(x, k):
        return lax.ppermute(x, "exp", [(j, j ^ k) for j in range(n_exp)])

    def per_device(tokens, phi, expert_out, slot_in_grad, out_grad):
        rows, width = tokens.shape
        slots = expert_out.shape[0]
        wide = width // n_exp
        half = phi.shape[0] // 2
        packed = jnp.concatenate([phi[:half], phi[half:]], axis=1)
        got_phi = gather_blocks(packed, "seq", n_seq)
        phi_full = jnp.concatenate([got_phi[:, :, :slots], got_phi[:, :, slots:]], axis=1)
        phi_full = phi_full.reshape(width, slots)

        logits = jnp.dot(tokens, phi_full, preferred_element_type=F32)
        disp_grad = lax.dot_general(
            tokens, slot_in_grad, (((1,), (1,)), ((), ())), preferred_element_type=F32
        )
        comb_grad = lax.dot_general(
            out_grad, expert_out, (((1,), (1,)), ((), ())), preferred_element_type=F32
        )

        rank = lax.axis_index("exp")
        place = jnp.stack([lax.rem(rank, GROUP), lax.div(rank, GROUP)]).astype(jnp.int32)
        weights = split_weights(place, slot_in_grad, phi_full, groups, wide)
        weights = [weights[0]] + [swap(weights[k], k) for k in range(1, GROUP)]

        row_top = jnp.max(logits, axis=1)
        row_exp = jnp.exp(logits - row_top[:, None])
        row_stats = jnp.stack(
            [row_top, jnp.sum(row_exp, axis=1), jnp.sum(row_exp * comb_grad, axis=1)]
        )
        col_top = jnp.max(logits, axis=0)
        col_exp = jnp.exp(logits - col_top[None, :])
        col_stats = jnp.stack(
            [col_top, jnp.sum(col_exp, axis=0), jnp.sum(col_exp * disp_grad, axis=0)]
        )

        col_stats = jnp.pad(col_stats, ((0, 0), (0, -slots % 128)))
        col_got = gather_blocks(col_stats, "seq", n_seq)
        row_stats, col_got, weights = lax.optimization_barrier((row_stats, col_got, weights))
        row_got = gather_blocks(row_stats, "exp", n_exp)
        col_peak, col_total, col_dot = merge_stats(col_got[:, :, :slots])
        row_peak, row_total, row_dot = merge_stats(row_got)

        combine = jnp.exp(logits - row_peak[:, None]) / row_total[:, None]
        dispatch = jnp.exp(logits - col_peak[None, :]) / col_total[None, :]
        combine_b = combine.astype(BF)
        logit_grad = (
            combine * (comb_grad - row_dot[:, None]) + dispatch * (disp_grad - col_dot[None, :])
        ).astype(BF)

        own = jnp.concatenate([dispatch.astype(BF), logit_grad], axis=1)
        own, logit_grad, combine_b = lax.optimization_barrier((own, logit_grad, combine_b))
        factors = [own] + [swap(own, k) for k in range(1, GROUP)]
        slot_term = lax.dot_general(
            out_grad, combine_b, (((0,), (0,)), ((), ())), preferred_element_type=F32
        ).astype(BF)

        phi_term = lax.dot_general(
            tokens, logit_grad, (((0,), (0,)), ((), ())), preferred_element_type=F32
        ).astype(BF)
        both = jnp.concatenate([phi_term, slot_term], axis=1)
        got = lax.all_to_all(both.reshape(n_seq, -1, 2 * slots), "seq", 0, 0, tiled=True)

        blocks = column_blocks(factors, weights, groups, wide)
        token_sum = blocks[0].astype(F32)
        for i in range(1, groups):
            turn = [(j, (j + i * GROUP) % n_exp) for j in range(n_exp)]
            token_sum = token_sum + lax.ppermute(blocks[i], "exp", turn).astype(F32)
        token_grad = token_sum.astype(BF)

        total = jnp.sum(got.astype(F32), axis=0)
        phi_grad = total[:, :slots]
        slot_grad = total[:, slots:].T.astype(BF)
        return (token_grad, phi_grad, slot_grad)

    return per_device


def solution(mesh):
    return jax.shard_map(
        make_per_device(mesh.shape["seq"], mesh.shape["exp"]),
        mesh=mesh,
        in_specs=(P("seq", None), P("seq", "exp"), P("exp", None), P("exp", None), P("seq", None)),
        out_specs=(P("seq", "exp"), P("seq", "exp"), P("exp", "seq")),
        check_vma=False,
    )
```

```python
import jax
import jax.numpy as jnp
from jax import lax
from jax.experimental import pallas as pl
from jax.experimental.pallas import tpu as pltpu
from jax.sharding import PartitionSpec as P

BF = jnp.bfloat16
F32 = jnp.float32
GROUP = 4


def gather_blocks(block, axis, n):
    spread = jnp.broadcast_to(block[None], (n,) + block.shape)
    return lax.all_to_all(spread, axis, 0, 0, tiled=True)


def merge_stats(got):
    peak, total, dot = got[:, 0], got[:, 1], got[:, 2]
    top = jnp.max(peak, axis=0)
    scale = jnp.exp(peak - top[None, :])
    total = jnp.sum(total * scale, axis=0)
    dot = jnp.sum(dot * scale, axis=0)
    return top, total, dot / total


def weights_kernel(place_ref, sig_ref, phi_ref, *out_refs):
    slots = sig_ref.shape[0]
    wide = out_refs[0].shape[1]
    for k, out_ref in enumerate(out_refs):
        block = jnp.bitwise_xor(place_ref[0], k)
        at = pl.ds(pl.multiple_of(block * wide, wide), wide)
        out_ref[:slots] = sig_ref[:, at]
        out_ref[slots:] = phi_ref[at, :].T


def split_weights(place, sig, phi_full, n, wide):
    slots, width = sig.shape
    spec = pl.BlockSpec((2 * slots, wide), lambda i, at: (0, i))
    return pl.pallas_call(
        weights_kernel,
        grid_spec=pltpu.PrefetchScalarGridSpec(
            num_scalar_prefetch=1,
            grid=(n,),
            in_specs=[
                pl.BlockSpec((slots, GROUP * wide), lambda i, at: (0, lax.rem(i + at[1], n))),
                pl.BlockSpec((GROUP * wide, slots), lambda i, at: (lax.rem(i + at[1], n), 0)),
            ],
            out_specs=[spec] * GROUP,
        ),
        out_shape=[jax.ShapeDtypeStruct((2 * slots, n * wide), BF)] * GROUP,
        cost_estimate=pl.CostEstimate(
            flops=4 * slots * width, bytes_accessed=8 * slots * width, transcendentals=0
        ),
        compiler_params=pltpu.CompilerParams(vmem_limit_bytes=32 * 1024 * 1024),
    )(place, sig, phi_full)


def blocks_kernel(*refs):
    factors, weights, out_refs = refs[:GROUP], refs[GROUP : 2 * GROUP], refs[2 * GROUP :]
    for i, out_ref in enumerate(out_refs):
        wide = out_ref.shape[1]
        at = slice(i * wide, (i + 1) * wide)
        acc = jnp.dot(factors[0][...], weights[0][:, at], preferred_element_type=F32)
        for f, w in zip(factors[1:], weights[1:]):
            acc = acc + jnp.dot(f[...], w[:, at], preferred_element_type=F32)
        out_ref[...] = acc.astype(BF)


def column_blocks(factors, weights, n, wide):
    rows, depth = factors[0].shape
    return pl.pallas_call(
        blocks_kernel,
        out_shape=[jax.ShapeDtypeStruct((rows, wide), BF)] * n,
        cost_estimate=pl.CostEstimate(
            flops=2 * GROUP * n * rows * depth * wide,
            bytes_accessed=2 * (GROUP * depth * (rows + n * wide) + n * rows * wide),
            transcendentals=0,
        ),
        compiler_params=pltpu.CompilerParams(vmem_limit_bytes=32 * 1024 * 1024),
    )(*factors, *weights)


def make_per_device(n_seq, n_exp):
    groups = n_exp // GROUP

    def swap(x, k):
        return lax.ppermute(x, "exp", [(j, j ^ k) for j in range(n_exp)])

    def per_device(tokens, phi, expert_out, slot_in_grad, out_grad):
        rows, width = tokens.shape
        slots = expert_out.shape[0]
        wide = width // n_exp
        half = phi.shape[0] // 2
        packed = jnp.concatenate([phi[:half], phi[half:]], axis=1)
        got_phi = gather_blocks(packed, "seq", n_seq)
        phi_full = jnp.concatenate([got_phi[:, :, :slots], got_phi[:, :, slots:]], axis=1)
        phi_full = phi_full.reshape(width, slots)

        logits = jnp.dot(tokens, phi_full, preferred_element_type=F32)
        disp_grad = lax.dot_general(
            tokens, slot_in_grad, (((1,), (1,)), ((), ())), preferred_element_type=F32
        )
        comb_grad = lax.dot_general(
            out_grad, expert_out, (((1,), (1,)), ((), ())), preferred_element_type=F32
        )

        rank = lax.axis_index("exp")
        place = jnp.stack([lax.rem(rank, GROUP), lax.div(rank, GROUP)]).astype(jnp.int32)
        weights = split_weights(place, slot_in_grad, phi_full, groups, wide)
        weights = [weights[0]] + [swap(weights[k], k) for k in range(1, GROUP)]

        row_top = jnp.max(logits, axis=1)
        row_exp = jnp.exp(logits - row_top[:, None])
        row_stats = jnp.stack(
            [row_top, jnp.sum(row_exp, axis=1), jnp.sum(row_exp * comb_grad, axis=1)]
        )
        col_top = jnp.max(logits, axis=0)
        col_exp = jnp.exp(logits - col_top[None, :])
        col_stats = jnp.stack(
            [col_top, jnp.sum(col_exp, axis=0), jnp.sum(col_exp * disp_grad, axis=0)]
        )

        row_got = gather_blocks(row_stats, "exp", n_exp)
        col_stats = jnp.pad(col_stats, ((0, 0), (0, -slots % 128)))
        spread = jnp.broadcast_to(col_stats[None], (n_seq,) + col_stats.shape)
        spread, row_got = lax.optimization_barrier((spread, row_got))
        col_got = lax.all_to_all(spread, "seq", 0, 0, tiled=True)
        col_got, weights = lax.optimization_barrier((col_got, weights))
        row_peak, row_total, row_dot = merge_stats(row_got)
        col_peak, col_total, col_dot = merge_stats(col_got[:, :, :slots])

        combine = jnp.exp(logits - row_peak[:, None]) / row_total[:, None]
        dispatch = jnp.exp(logits - col_peak[None, :]) / col_total[None, :]
        combine_b = combine.astype(BF)
        logit_grad = (
            combine * (comb_grad - row_dot[:, None]) + dispatch * (disp_grad - col_dot[None, :])
        ).astype(BF)

        own = jnp.concatenate([dispatch.astype(BF), logit_grad], axis=1)
        own, logit_grad, combine_b = lax.optimization_barrier((own, logit_grad, combine_b))
        factors = [own] + [swap(own, k) for k in range(1, GROUP)]
        slot_term = lax.dot_general(
            out_grad, combine_b, (((0,), (0,)), ((), ())), preferred_element_type=F32
        ).astype(BF)

        phi_term = lax.dot_general(
            tokens, logit_grad, (((0,), (0,)), ((), ())), preferred_element_type=F32
        ).astype(BF)
        both = jnp.concatenate([phi_term, slot_term], axis=1)
        got = lax.all_to_all(both.reshape(n_seq, -1, 2 * slots), "seq", 0, 0, tiled=True)

        blocks = column_blocks(factors, weights, groups, wide)
        token_sum = blocks[0].astype(F32)
        for i in sorted(range(1, groups), key=lambda i: abs(2 * i - groups)):
            turn = [(j, (j + i * GROUP) % n_exp) for j in range(n_exp)]
            token_sum = token_sum + lax.ppermute(blocks[i], "exp", turn).astype(F32)
        token_grad = token_sum.astype(BF)

        total = jnp.sum(got.astype(F32), axis=0)
        phi_grad = total[:, :slots]
        slot_grad = total[:, slots:].T.astype(BF)
        return (token_grad, phi_grad, slot_grad)

    return per_device


def solution(mesh):
    return jax.shard_map(
        make_per_device(mesh.shape["seq"], mesh.shape["exp"]),
        mesh=mesh,
        in_specs=(P("seq", None), P("seq", "exp"), P("exp", None), P("exp", None), P("seq", None)),
        out_specs=(P("seq", "exp"), P("seq", "exp"), P("exp", "seq")),
        check_vma=False,
    )
```

```python
import jax
import jax.numpy as jnp
from jax import lax
from jax.experimental import pallas as pl
from jax.experimental.pallas import tpu as pltpu
from jax.sharding import Mesh
from jax.sharding import PartitionSpec as P

BF = jnp.bfloat16
F32 = jnp.float32
SEQ = ("chip", "core")
GROUP = 4


def gather_blocks(block, axis, n):
    spread = jnp.broadcast_to(block[None], (n,) + block.shape)
    return lax.all_to_all(spread, axis, 0, 0, tiled=True)


def merge_stats(got):
    peak, total, dot = got[:, 0], got[:, 1], got[:, 2]
    top = jnp.max(peak, axis=0)
    scale = jnp.exp(peak - top[None, :])
    total = jnp.sum(total * scale, axis=0)
    dot = jnp.sum(dot * scale, axis=0)
    return top, total, dot / total


def weights_kernel(place_ref, sig_ref, phi_ref, *out_refs):
    slots = sig_ref.shape[0]
    wide = out_refs[0].shape[1]
    for k, out_ref in enumerate(out_refs):
        block = jnp.bitwise_xor(place_ref[0], k)
        at = pl.ds(pl.multiple_of(block * wide, wide), wide)
        out_ref[:slots] = sig_ref[:, at]
        out_ref[slots:] = phi_ref[at, :].T


def split_weights(place, sig, phi_full, n, wide):
    slots, width = sig.shape
    spec = pl.BlockSpec((2 * slots, wide), lambda i, at: (0, i))
    return pl.pallas_call(
        weights_kernel,
        grid_spec=pltpu.PrefetchScalarGridSpec(
            num_scalar_prefetch=1,
            grid=(n,),
            in_specs=[
                pl.BlockSpec((slots, GROUP * wide), lambda i, at: (0, lax.rem(i + at[1], n))),
                pl.BlockSpec((GROUP * wide, slots), lambda i, at: (lax.rem(i + at[1], n), 0)),
            ],
            out_specs=[spec] * GROUP,
        ),
        out_shape=[jax.ShapeDtypeStruct((2 * slots, n * wide), BF)] * GROUP,
        cost_estimate=pl.CostEstimate(
            flops=4 * slots * width, bytes_accessed=8 * slots * width, transcendentals=0
        ),
        compiler_params=pltpu.CompilerParams(vmem_limit_bytes=32 * 1024 * 1024),
    )(place, sig, phi_full)


def blocks_kernel(*refs):
    factors, weights, out_refs = refs[:GROUP], refs[GROUP : 2 * GROUP], refs[2 * GROUP :]
    for i, out_ref in enumerate(out_refs):
        wide = out_ref.shape[1]
        at = slice(i * wide, (i + 1) * wide)
        acc = jnp.dot(factors[0][...], weights[0][:, at], preferred_element_type=F32)
        for f, w in zip(factors[1:], weights[1:]):
            acc = acc + jnp.dot(f[...], w[:, at], preferred_element_type=F32)
        out_ref[...] = acc.astype(BF)


def column_blocks(factors, weights, n, wide):
    rows, depth = factors[0].shape
    return pl.pallas_call(
        blocks_kernel,
        out_shape=[jax.ShapeDtypeStruct((rows, wide), BF)] * n,
        cost_estimate=pl.CostEstimate(
            flops=2 * GROUP * n * rows * depth * wide,
            bytes_accessed=2 * (GROUP * depth * (rows + n * wide) + n * rows * wide),
            transcendentals=0,
        ),
        compiler_params=pltpu.CompilerParams(vmem_limit_bytes=32 * 1024 * 1024),
    )(*factors, *weights)


def make_per_device(n_seq, n_exp):
    groups = n_exp // GROUP

    def swap(x, k):
        return lax.ppermute(x, "exp", [(j, j ^ k) for j in range(n_exp)])

    def per_device(tokens, phi, expert_out, slot_in_grad, out_grad):
        rows, width = tokens.shape
        slots = expert_out.shape[0]
        wide = width // n_exp
        half = phi.shape[0] // 2
        packed = jnp.concatenate([phi[:half], phi[half:]], axis=1)
        got_phi = gather_blocks(packed, SEQ, n_seq)
        phi_full = jnp.concatenate([got_phi[:, :, :slots], got_phi[:, :, slots:]], axis=1)
        phi_full = phi_full.reshape(width, slots)

        logits = jnp.dot(tokens, phi_full, preferred_element_type=F32)
        disp_grad = lax.dot_general(
            tokens, slot_in_grad, (((1,), (1,)), ((), ())), preferred_element_type=F32
        )
        comb_grad = lax.dot_general(
            out_grad, expert_out, (((1,), (1,)), ((), ())), preferred_element_type=F32
        )

        rank = lax.axis_index("exp")
        place = jnp.stack([lax.rem(rank, GROUP), lax.div(rank, GROUP)]).astype(jnp.int32)
        weights = split_weights(place, slot_in_grad, phi_full, groups, wide)
        weights = [weights[0]] + [swap(weights[k], k) for k in range(1, GROUP)]

        row_top = jnp.max(logits, axis=1)
        row_exp = jnp.exp(logits - row_top[:, None])
        row_stats = jnp.stack(
            [row_top, jnp.sum(row_exp, axis=1), jnp.sum(row_exp * comb_grad, axis=1)]
        )
        col_top = jnp.max(logits, axis=0)
        col_exp = jnp.exp(logits - col_top[None, :])
        col_stats = jnp.stack(
            [col_top, jnp.sum(col_exp, axis=0), jnp.sum(col_exp * disp_grad, axis=0)]
        )

        row_got = gather_blocks(row_stats, "exp", n_exp)
        col_stats = jnp.pad(col_stats, ((0, 0), (0, -slots % 128)))
        spread = jnp.broadcast_to(col_stats[None], (n_seq,) + col_stats.shape)
        spread, row_got = lax.optimization_barrier((spread, row_got))
        col_got = lax.all_to_all(spread, SEQ, 0, 0, tiled=True)
        col_got, weights = lax.optimization_barrier((col_got, weights))
        row_peak, row_total, row_dot = merge_stats(row_got)
        col_peak, col_total, col_dot = merge_stats(col_got[:, :, :slots])

        combine = jnp.exp(logits - row_peak[:, None]) / row_total[:, None]
        dispatch = jnp.exp(logits - col_peak[None, :]) / col_total[None, :]
        combine_b = combine.astype(BF)
        logit_grad = (
            combine * (comb_grad - row_dot[:, None]) + dispatch * (disp_grad - col_dot[None, :])
        ).astype(BF)

        own = jnp.concatenate([dispatch.astype(BF), logit_grad], axis=1)
        own, logit_grad, combine_b = lax.optimization_barrier((own, logit_grad, combine_b))
        factors = [own] + [swap(own, k) for k in range(1, GROUP)]
        slot_term = lax.dot_general(
            out_grad, combine_b, (((0,), (0,)), ((), ())), preferred_element_type=F32
        ).astype(BF)

        phi_term = lax.dot_general(
            tokens, logit_grad, (((0,), (0,)), ((), ())), preferred_element_type=F32
        ).astype(BF)
        both = jnp.concatenate([phi_term, slot_term], axis=1)
        pairs = both.reshape(n_seq // 2, 2, -1, 2 * slots)
        first = lax.axis_index("core") == 0
        kept = jnp.where(first, pairs[:, 0], pairs[:, 1])
        lent = jnp.where(first, pairs[:, 1], pairs[:, 0])
        lent = lax.ppermute(lent, "core", [(0, 1), (1, 0)])
        pair_sum = (kept.astype(F32) + lent.astype(F32)).astype(BF)
        pair_sum, factors = lax.optimization_barrier((pair_sum, factors))
        got = lax.all_to_all(pair_sum, "chip", 0, 0, tiled=True)

        blocks = column_blocks(factors, weights, groups, wide)
        token_sum = blocks[0].astype(F32)
        for i in sorted(range(1, groups), key=lambda i: abs(2 * i - groups)):
            turn = [(j, (j + i * GROUP) % n_exp) for j in range(n_exp)]
            token_sum = token_sum + lax.ppermute(blocks[i], "exp", turn).astype(F32)
        token_grad = token_sum.astype(BF)

        total = jnp.sum(got.astype(F32), axis=0)
        phi_grad = total[:, :slots]
        slot_grad = total[:, slots:].T.astype(BF)
        return (token_grad, phi_grad, slot_grad)

    return per_device


def solution(mesh):
    n_seq, n_exp = mesh.devices.shape
    fine = Mesh(mesh.devices.reshape(n_seq // 2, 2, n_exp), ("chip", "core", "exp"))
    return jax.shard_map(
        make_per_device(n_seq, n_exp),
        mesh=fine,
        in_specs=(P(SEQ, None), P(SEQ, "exp"), P("exp", None), P("exp", None), P(SEQ, None)),
        out_specs=(P(SEQ, "exp"), P(SEQ, "exp"), P("exp", SEQ)),
        check_vma=False,
    )
```

```python
import jax
import jax.numpy as jnp
from jax import lax
from jax.experimental import pallas as pl
from jax.experimental.pallas import tpu as pltpu
from jax.sharding import PartitionSpec as P

BF = jnp.bfloat16
F32 = jnp.float32
GROUP = 4


def gather_blocks(block, axis, n):
    spread = jnp.broadcast_to(block[None], (n,) + block.shape)
    return lax.all_to_all(spread, axis, 0, 0, tiled=True)


def merge_stats(got):
    peak, total, dot = got[:, 0], got[:, 1], got[:, 2]
    top = jnp.max(peak, axis=0)
    scale = jnp.exp(peak - top[None, :])
    total = jnp.sum(total * scale, axis=0)
    dot = jnp.sum(dot * scale, axis=0)
    return top, total, dot / total


def copies_kernel(block_ref, out_ref):
    half = block_ref.shape[0] // 2
    packed = jnp.concatenate([block_ref[:half], block_ref[half:]], axis=1)
    out_ref[...] = jnp.broadcast_to(packed[None], out_ref.shape)


def packed_copies(block, n):
    rows, width = block.shape
    return pl.pallas_call(
        copies_kernel,
        out_shape=jax.ShapeDtypeStruct((n, rows // 2, 2 * width), block.dtype),
        cost_estimate=pl.CostEstimate(
            flops=0, bytes_accessed=2 * (n + 1) * rows * width, transcendentals=0
        ),
    )(block)


def weights_kernel(place_ref, sig_ref, phi_ref, *out_refs):
    slots = sig_ref.shape[0]
    wide = out_refs[0].shape[1]
    for k, out_ref in enumerate(out_refs):
        block = jnp.bitwise_xor(place_ref[0], k)
        at = pl.ds(pl.multiple_of(block * wide, wide), wide)
        out_ref[:slots] = sig_ref[:, at]
        out_ref[slots:] = phi_ref[at, :].T


def split_weights(place, sig, phi_full, n, wide):
    slots, width = sig.shape
    spec = pl.BlockSpec((2 * slots, wide), lambda i, at: (0, i))
    return pl.pallas_call(
        weights_kernel,
        grid_spec=pltpu.PrefetchScalarGridSpec(
            num_scalar_prefetch=1,
            grid=(n,),
            in_specs=[
                pl.BlockSpec((slots, GROUP * wide), lambda i, at: (0, lax.rem(i + at[1], n))),
                pl.BlockSpec((GROUP * wide, slots), lambda i, at: (lax.rem(i + at[1], n), 0)),
            ],
            out_specs=[spec] * GROUP,
        ),
        out_shape=[jax.ShapeDtypeStruct((2 * slots, n * wide), BF)] * GROUP,
        cost_estimate=pl.CostEstimate(
            flops=4 * slots * width, bytes_accessed=8 * slots * width, transcendentals=0
        ),
        compiler_params=pltpu.CompilerParams(vmem_limit_bytes=32 * 1024 * 1024),
    )(place, sig, phi_full)


def blocks_kernel(*refs):
    factors, weights, out_refs = refs[:GROUP], refs[GROUP : 2 * GROUP], refs[2 * GROUP :]
    for i, out_ref in enumerate(out_refs):
        wide = out_ref.shape[1]
        at = slice(i * wide, (i + 1) * wide)
        acc = jnp.dot(factors[0][...], weights[0][:, at], preferred_element_type=F32)
        for f, w in zip(factors[1:], weights[1:]):
            acc = acc + jnp.dot(f[...], w[:, at], preferred_element_type=F32)
        out_ref[...] = acc.astype(BF)


def column_blocks(factors, weights, n, wide):
    rows, depth = factors[0].shape
    return pl.pallas_call(
        blocks_kernel,
        out_shape=[jax.ShapeDtypeStruct((rows, wide), BF)] * n,
        cost_estimate=pl.CostEstimate(
            flops=2 * GROUP * n * rows * depth * wide,
            bytes_accessed=2 * (GROUP * depth * (rows + n * wide) + n * rows * wide),
            transcendentals=0,
        ),
        compiler_params=pltpu.CompilerParams(vmem_limit_bytes=32 * 1024 * 1024),
    )(*factors, *weights)


def make_per_device(n_seq, n_exp):
    groups = n_exp // GROUP

    def swap(x, k):
        return lax.ppermute(x, "exp", [(j, j ^ k) for j in range(n_exp)])

    def per_device(tokens, phi, expert_out, slot_in_grad, out_grad):
        rows, width = tokens.shape
        slots = expert_out.shape[0]
        wide = width // n_exp
        got_phi = lax.all_to_all(packed_copies(phi, n_seq), "seq", 0, 0, tiled=True)
        phi_full = jnp.concatenate([got_phi[:, :, :slots], got_phi[:, :, slots:]], axis=1)
        phi_full = phi_full.reshape(width, slots)

        logits = jnp.dot(tokens, phi_full, preferred_element_type=F32)
        disp_grad = lax.dot_general(
            tokens, slot_in_grad, (((1,), (1,)), ((), ())), preferred_element_type=F32
        )
        comb_grad = lax.dot_general(
            out_grad, expert_out, (((1,), (1,)), ((), ())), preferred_element_type=F32
        )

        rank = lax.axis_index("exp")
        place = jnp.stack([lax.rem(rank, GROUP), lax.div(rank, GROUP)]).astype(jnp.int32)
        weights = split_weights(place, slot_in_grad, phi_full, groups, wide)
        weights = [weights[0]] + [swap(weights[k], k) for k in range(1, GROUP)]

        row_top = jnp.max(logits, axis=1)
        row_exp = jnp.exp(logits - row_top[:, None])
        row_stats = jnp.stack(
            [row_top, jnp.sum(row_exp, axis=1), jnp.sum(row_exp * comb_grad, axis=1)]
        )
        col_top = jnp.max(logits, axis=0)
        col_exp = jnp.exp(logits - col_top[None, :])
        col_stats = jnp.stack(
            [col_top, jnp.sum(col_exp, axis=0), jnp.sum(col_exp * disp_grad, axis=0)]
        )

        row_got = gather_blocks(row_stats, "exp", n_exp)
        col_stats = jnp.pad(col_stats, ((0, 0), (0, -slots % 128)))
        spread = jnp.broadcast_to(col_stats[None], (n_seq,) + col_stats.shape)
        spread, row_got, weights = lax.optimization_barrier((spread, row_got, weights))
        col_got = lax.all_to_all(spread, "seq", 0, 0, tiled=True)
        row_peak, row_total, row_dot = merge_stats(row_got)
        col_peak, col_total, col_dot = merge_stats(col_got[:, :, :slots])

        combine = jnp.exp(logits - row_peak[:, None]) / row_total[:, None]
        dispatch = jnp.exp(logits - col_peak[None, :]) / col_total[None, :]
        combine_b = combine.astype(BF)
        logit_grad = (
            combine * (comb_grad - row_dot[:, None]) + dispatch * (disp_grad - col_dot[None, :])
        ).astype(BF)

        own = jnp.concatenate([dispatch.astype(BF), logit_grad], axis=1)
        own, logit_grad, combine_b = lax.optimization_barrier((own, logit_grad, combine_b))
        factors = [own] + [swap(own, k) for k in range(1, GROUP)]
        slot_term = lax.dot_general(
            out_grad, combine_b, (((0,), (0,)), ((), ())), preferred_element_type=F32
        ).astype(BF)

        phi_term = lax.dot_general(
            tokens, logit_grad, (((0,), (0,)), ((), ())), preferred_element_type=F32
        ).astype(BF)
        both = jnp.concatenate([phi_term, slot_term], axis=1)
        got = lax.all_to_all(both.reshape(n_seq, -1, 2 * slots), "seq", 0, 0, tiled=True)

        blocks = column_blocks(factors, weights, groups, wide)
        token_sum = blocks[0].astype(F32)
        for i in sorted(range(1, groups), key=lambda i: abs(2 * i - groups)):
            turn = [(j, (j + i * GROUP) % n_exp) for j in range(n_exp)]
            token_sum = token_sum + lax.ppermute(blocks[i], "exp", turn).astype(F32)
        token_grad = token_sum.astype(BF)

        total = jnp.sum(got.astype(F32), axis=0)
        phi_grad = total[:, :slots]
        slot_grad = total[:, slots:].T.astype(BF)
        return (token_grad, phi_grad, slot_grad)

    return per_device


def solution(mesh):
    return jax.shard_map(
        make_per_device(mesh.shape["seq"], mesh.shape["exp"]),
        mesh=mesh,
        in_specs=(P("seq", None), P("seq", "exp"), P("exp", None), P("exp", None), P("seq", None)),
        out_specs=(P("seq", "exp"), P("seq", "exp"), P("exp", "seq")),
        check_vma=False,
    )
```

```python
import jax
import jax.numpy as jnp
from jax import lax
from jax.experimental import pallas as pl
from jax.experimental.pallas import tpu as pltpu
from jax.sharding import PartitionSpec as P

BF = jnp.bfloat16
F32 = jnp.float32
GROUP = 4


def gather_blocks(block, axis, n):
    spread = jnp.broadcast_to(block[None], (n,) + block.shape)
    return lax.all_to_all(spread, axis, 0, 0, tiled=True)


def merge_stats(got):
    peak, total, dot = got[:, 0], got[:, 1], got[:, 2]
    top = jnp.max(peak, axis=0)
    scale = jnp.exp(peak - top[None, :])
    total = jnp.sum(total * scale, axis=0)
    dot = jnp.sum(dot * scale, axis=0)
    return top, total, dot / total


def copies_kernel(block_ref, out_ref):
    half = block_ref.shape[0] // 2
    packed = jnp.concatenate([block_ref[:half], block_ref[half:]], axis=1)
    out_ref[...] = jnp.broadcast_to(packed[None], out_ref.shape)


def packed_copies(block, n):
    rows, width = block.shape
    return pl.pallas_call(
        copies_kernel,
        out_shape=jax.ShapeDtypeStruct((n, rows // 2, 2 * width), block.dtype),
        cost_estimate=pl.CostEstimate(
            flops=0, bytes_accessed=2 * (n + 1) * rows * width, transcendentals=0
        ),
    )(block)


def weights_kernel(place_ref, sig_ref, phi_ref, *out_refs):
    slots = sig_ref.shape[0]
    wide = out_refs[0].shape[1]
    for k, out_ref in enumerate(out_refs):
        block = jnp.bitwise_xor(place_ref[0], k)
        at = pl.ds(pl.multiple_of(block * wide, wide), wide)
        out_ref[:slots] = sig_ref[:, at]
        out_ref[slots:] = phi_ref[at, :].T


def split_weights(place, sig, phi_full, n, wide):
    slots, width = sig.shape
    spec = pl.BlockSpec((2 * slots, wide), lambda i, at: (0, i))
    return pl.pallas_call(
        weights_kernel,
        grid_spec=pltpu.PrefetchScalarGridSpec(
            num_scalar_prefetch=1,
            grid=(n,),
            in_specs=[
                pl.BlockSpec((slots, GROUP * wide), lambda i, at: (0, lax.rem(i + at[1], n))),
                pl.BlockSpec((GROUP * wide, slots), lambda i, at: (lax.rem(i + at[1], n), 0)),
            ],
            out_specs=[spec] * GROUP,
        ),
        out_shape=[jax.ShapeDtypeStruct((2 * slots, n * wide), BF)] * GROUP,
        cost_estimate=pl.CostEstimate(
            flops=4 * slots * width, bytes_accessed=8 * slots * width, transcendentals=0
        ),
        compiler_params=pltpu.CompilerParams(vmem_limit_bytes=32 * 1024 * 1024),
    )(place, sig, phi_full)


def blocks_kernel(*refs):
    factors, weights, out_refs = refs[:GROUP], refs[GROUP : 2 * GROUP], refs[2 * GROUP :]
    for i, out_ref in enumerate(out_refs):
        wide = out_ref.shape[1]
        at = slice(i * wide, (i + 1) * wide)
        acc = jnp.dot(factors[0][...], weights[0][:, at], preferred_element_type=F32)
        for f, w in zip(factors[1:], weights[1:]):
            acc = acc + jnp.dot(f[...], w[:, at], preferred_element_type=F32)
        out_ref[...] = acc.astype(BF)


def column_blocks(factors, weights, n, wide):
    rows, depth = factors[0].shape
    return pl.pallas_call(
        blocks_kernel,
        out_shape=[jax.ShapeDtypeStruct((rows, wide), BF)] * n,
        cost_estimate=pl.CostEstimate(
            flops=2 * GROUP * n * rows * depth * wide,
            bytes_accessed=2 * (GROUP * depth * (rows + n * wide) + n * rows * wide),
            transcendentals=0,
        ),
        compiler_params=pltpu.CompilerParams(vmem_limit_bytes=32 * 1024 * 1024),
    )(*factors, *weights)


def make_per_device(n_seq, n_exp):
    groups = n_exp // GROUP

    def swap(x, k):
        return lax.ppermute(x, "exp", [(j, j ^ k) for j in range(n_exp)])

    def per_device(tokens, phi, expert_out, slot_in_grad, out_grad):
        rows, width = tokens.shape
        slots = expert_out.shape[0]
        wide = width // n_exp
        got_phi = lax.all_to_all(packed_copies(phi, n_seq), "seq", 0, 0, tiled=True)
        phi_full = jnp.concatenate([got_phi[:, :, :slots], got_phi[:, :, slots:]], axis=1)
        phi_full = phi_full.reshape(width, slots)

        logits = jnp.dot(tokens, phi_full, preferred_element_type=F32)
        disp_grad = lax.dot_general(
            tokens, slot_in_grad, (((1,), (1,)), ((), ())), preferred_element_type=F32
        )
        comb_grad = lax.dot_general(
            out_grad, expert_out, (((1,), (1,)), ((), ())), preferred_element_type=F32
        )

        rank = lax.axis_index("exp")
        place = jnp.stack([lax.rem(rank, GROUP), lax.div(rank, GROUP)]).astype(jnp.int32)
        weights = split_weights(place, slot_in_grad, phi_full, groups, wide)
        weights = list(weights)
        lent = weights[1:]
        weights[1] = swap(lent[0], 1)

        row_top = jnp.max(logits, axis=1)
        row_exp = jnp.exp(logits - row_top[:, None])
        row_stats = jnp.stack(
            [row_top, jnp.sum(row_exp, axis=1), jnp.sum(row_exp * comb_grad, axis=1)]
        )
        col_top = jnp.max(logits, axis=0)
        col_exp = jnp.exp(logits - col_top[None, :])
        col_stats = jnp.stack(
            [col_top, jnp.sum(col_exp, axis=0), jnp.sum(col_exp * disp_grad, axis=0)]
        )

        row_got = gather_blocks(row_stats, "exp", n_exp)
        col_stats = jnp.pad(col_stats, ((0, 0), (0, -slots % 128)))
        spread = jnp.broadcast_to(col_stats[None], (n_seq,) + col_stats.shape)
        spread, row_got, lent, weights[1] = lax.optimization_barrier(
            (spread, row_got, lent, weights[1])
        )
        col_got = lax.all_to_all(spread, "seq", 0, 0, tiled=True)
        for k in range(2, GROUP):
            weights[k] = swap(lent[k - 1], k)
        col_got, weights = lax.optimization_barrier((col_got, weights))
        row_peak, row_total, row_dot = merge_stats(row_got)
        col_peak, col_total, col_dot = merge_stats(col_got[:, :, :slots])

        combine = jnp.exp(logits - row_peak[:, None]) / row_total[:, None]
        dispatch = jnp.exp(logits - col_peak[None, :]) / col_total[None, :]
        combine_b = combine.astype(BF)
        logit_grad = (
            combine * (comb_grad - row_dot[:, None]) + dispatch * (disp_grad - col_dot[None, :])
        ).astype(BF)

        own = jnp.concatenate([dispatch.astype(BF), logit_grad], axis=1)
        own, logit_grad, combine_b = lax.optimization_barrier((own, logit_grad, combine_b))
        factors = [own] + [swap(own, k) for k in range(1, GROUP)]
        slot_term = lax.dot_general(
            out_grad, combine_b, (((0,), (0,)), ((), ())), preferred_element_type=F32
        ).astype(BF)

        phi_term = lax.dot_general(
            tokens, logit_grad, (((0,), (0,)), ((), ())), preferred_element_type=F32
        ).astype(BF)
        both = jnp.concatenate([phi_term, slot_term], axis=1)
        got = lax.all_to_all(both.reshape(n_seq, -1, 2 * slots), "seq", 0, 0, tiled=True)

        blocks = column_blocks(factors, weights, groups, wide)
        token_sum = blocks[0].astype(F32)
        for i in sorted(range(1, groups), key=lambda i: abs(2 * i - groups)):
            turn = [(j, (j + i * GROUP) % n_exp) for j in range(n_exp)]
            token_sum = token_sum + lax.ppermute(blocks[i], "exp", turn).astype(F32)
        token_grad = token_sum.astype(BF)

        total = jnp.sum(got.astype(F32), axis=0)
        phi_grad = total[:, :slots]
        slot_grad = total[:, slots:].T.astype(BF)
        return (token_grad, phi_grad, slot_grad)

    return per_device


def solution(mesh):
    return jax.shard_map(
        make_per_device(mesh.shape["seq"], mesh.shape["exp"]),
        mesh=mesh,
        in_specs=(P("seq", None), P("seq", "exp"), P("exp", None), P("exp", None), P("seq", None)),
        out_specs=(P("seq", "exp"), P("seq", "exp"), P("exp", "seq")),
        check_vma=False,
    )
```

```python
import jax
import jax.numpy as jnp
from jax import lax
from jax.experimental import pallas as pl
from jax.experimental.pallas import tpu as pltpu
from jax.sharding import PartitionSpec as P

BF = jnp.bfloat16
F32 = jnp.float32
GROUP = 4


def gather_blocks(block, axis, n):
    spread = jnp.broadcast_to(block[None], (n,) + block.shape)
    return lax.all_to_all(spread, axis, 0, 0, tiled=True)


def merge_stats(got):
    peak, total, dot = got[:, 0], got[:, 1], got[:, 2]
    top = jnp.max(peak, axis=0)
    scale = jnp.exp(peak - top[None, :])
    total = jnp.sum(total * scale, axis=0)
    dot = jnp.sum(dot * scale, axis=0)
    return top, total, dot / total


def copies_kernel(block_ref, out_ref):
    half = block_ref.shape[0] // 2
    packed = jnp.concatenate([block_ref[:half], block_ref[half:]], axis=1)
    out_ref[...] = jnp.broadcast_to(packed[None], out_ref.shape)


def packed_copies(block, n):
    rows, width = block.shape
    return pl.pallas_call(
        copies_kernel,
        out_shape=jax.ShapeDtypeStruct((n, rows // 2, 2 * width), block.dtype),
        cost_estimate=pl.CostEstimate(
            flops=0, bytes_accessed=2 * (n + 1) * rows * width, transcendentals=0
        ),
    )(block)


def weights_kernel(place_ref, sig_ref, phi_ref, *out_refs):
    slots = sig_ref.shape[0]
    wide = out_refs[0].shape[1]
    for k, out_ref in enumerate(out_refs):
        block = jnp.bitwise_xor(place_ref[0], k)
        at = pl.ds(pl.multiple_of(block * wide, wide), wide)
        out_ref[:slots] = sig_ref[:, at]
        out_ref[slots:] = phi_ref[at, :].T


def split_weights(place, sig, phi_full, n, wide):
    slots, width = sig.shape
    spec = pl.BlockSpec((2 * slots, wide), lambda i, at: (0, i))
    return pl.pallas_call(
        weights_kernel,
        grid_spec=pltpu.PrefetchScalarGridSpec(
            num_scalar_prefetch=1,
            grid=(n,),
            in_specs=[
                pl.BlockSpec((slots, GROUP * wide), lambda i, at: (0, lax.rem(i + at[1], n))),
                pl.BlockSpec((GROUP * wide, slots), lambda i, at: (lax.rem(i + at[1], n), 0)),
            ],
            out_specs=[spec] * GROUP,
        ),
        out_shape=[jax.ShapeDtypeStruct((2 * slots, n * wide), BF)] * GROUP,
        cost_estimate=pl.CostEstimate(
            flops=4 * slots * width, bytes_accessed=8 * slots * width, transcendentals=0
        ),
        compiler_params=pltpu.CompilerParams(vmem_limit_bytes=32 * 1024 * 1024),
    )(place, sig, phi_full)


def blocks_kernel(*refs):
    factors, weights, out_refs = refs[:GROUP], refs[GROUP : 2 * GROUP], refs[2 * GROUP :]
    for i, out_ref in enumerate(out_refs):
        wide = out_ref.shape[1]
        at = slice(i * wide, (i + 1) * wide)
        acc = jnp.dot(factors[0][...], weights[0][:, at], preferred_element_type=F32)
        for f, w in zip(factors[1:], weights[1:]):
            acc = acc + jnp.dot(f[...], w[:, at], preferred_element_type=F32)
        out_ref[...] = acc.astype(BF)


def column_blocks(factors, weights, n, wide):
    rows, depth = factors[0].shape
    return pl.pallas_call(
        blocks_kernel,
        out_shape=[jax.ShapeDtypeStruct((rows, wide), BF)] * n,
        cost_estimate=pl.CostEstimate(
            flops=2 * GROUP * n * rows * depth * wide,
            bytes_accessed=2 * (GROUP * depth * (rows + n * wide) + n * rows * wide),
            transcendentals=0,
        ),
        compiler_params=pltpu.CompilerParams(vmem_limit_bytes=32 * 1024 * 1024),
    )(*factors, *weights)


def make_per_device(n_seq, n_exp):
    groups = n_exp // GROUP

    def swap(x, k):
        return lax.ppermute(x, "exp", [(j, j ^ k) for j in range(n_exp)])

    def per_device(tokens, phi, expert_out, slot_in_grad, out_grad):
        rows, width = tokens.shape
        slots = expert_out.shape[0]
        wide = width // n_exp
        got_phi = lax.all_to_all(packed_copies(phi, n_seq), "seq", 0, 0, tiled=True)
        phi_full = jnp.concatenate([got_phi[:, :, :slots], got_phi[:, :, slots:]], axis=1)
        phi_full = phi_full.reshape(width, slots)

        logits = jnp.dot(tokens, phi_full, preferred_element_type=F32)
        disp_grad = lax.dot_general(
            tokens, slot_in_grad, (((1,), (1,)), ((), ())), preferred_element_type=F32
        )
        comb_grad = lax.dot_general(
            out_grad, expert_out, (((1,), (1,)), ((), ())), preferred_element_type=F32
        )

        rank = lax.axis_index("exp")
        place = jnp.stack([lax.rem(rank, GROUP), lax.div(rank, GROUP)]).astype(jnp.int32)
        weights = split_weights(place, slot_in_grad, phi_full, groups, wide)

        row_top = jnp.max(logits, axis=1)
        row_exp = jnp.exp(logits - row_top[:, None])
        row_stats = jnp.stack(
            [row_top, jnp.sum(row_exp, axis=1), jnp.sum(row_exp * comb_grad, axis=1)]
        )
        col_top = jnp.max(logits, axis=0)
        col_exp = jnp.exp(logits - col_top[None, :])
        col_stats = jnp.stack(
            [col_top, jnp.sum(col_exp, axis=0), jnp.sum(col_exp * disp_grad, axis=0)]
        )

        row_got = gather_blocks(row_stats, "exp", n_exp)
        col_stats = jnp.pad(col_stats, ((0, 0), (0, -slots % 128)))
        spread = jnp.broadcast_to(col_stats[None], (n_seq,) + col_stats.shape)
        spread, row_got, weights = lax.optimization_barrier((spread, row_got, weights))
        col_got = lax.all_to_all(spread, "seq", 0, 0, tiled=True)
        weights = [weights[0]] + [swap(weights[k], k) for k in range(GROUP - 1, 0, -1)][::-1]
        col_got, weights = lax.optimization_barrier((col_got, weights))
        row_peak, row_total, row_dot = merge_stats(row_got)
        col_peak, col_total, col_dot = merge_stats(col_got[:, :, :slots])

        combine = jnp.exp(logits - row_peak[:, None]) / row_total[:, None]
        dispatch = jnp.exp(logits - col_peak[None, :]) / col_total[None, :]
        combine_b = combine.astype(BF)
        logit_grad = (
            combine * (comb_grad - row_dot[:, None]) + dispatch * (disp_grad - col_dot[None, :])
        ).astype(BF)

        own = jnp.concatenate([dispatch.astype(BF), logit_grad], axis=1)
        own, logit_grad, combine_b = lax.optimization_barrier((own, logit_grad, combine_b))
        factors = [own] + [swap(own, k) for k in range(1, GROUP)]
        slot_term = lax.dot_general(
            out_grad, combine_b, (((0,), (0,)), ((), ())), preferred_element_type=F32
        ).astype(BF)

        phi_term = lax.dot_general(
            tokens, logit_grad, (((0,), (0,)), ((), ())), preferred_element_type=F32
        ).astype(BF)
        both = jnp.concatenate([phi_term, slot_term], axis=1)
        got = lax.all_to_all(both.reshape(n_seq, -1, 2 * slots), "seq", 0, 0, tiled=True)

        blocks = column_blocks(factors, weights, groups, wide)
        token_sum = blocks[0].astype(F32)
        for i in sorted(range(1, groups), key=lambda i: abs(2 * i - groups)):
            turn = [(j, (j + i * GROUP) % n_exp) for j in range(n_exp)]
            token_sum = token_sum + lax.ppermute(blocks[i], "exp", turn).astype(F32)
        token_grad = token_sum.astype(BF)

        total = jnp.sum(got.astype(F32), axis=0)
        phi_grad = total[:, :slots]
        slot_grad = total[:, slots:].T.astype(BF)
        return (token_grad, phi_grad, slot_grad)

    return per_device


def solution(mesh):
    return jax.shard_map(
        make_per_device(mesh.shape["seq"], mesh.shape["exp"]),
        mesh=mesh,
        in_specs=(P("seq", None), P("seq", "exp"), P("exp", None), P("exp", None), P("seq", None)),
        out_specs=(P("seq", "exp"), P("seq", "exp"), P("exp", "seq")),
        check_vma=False,
    )
```
